32 devices in a mesh: groups: 2 (over x), tensor: 16 (over z, y, core).
Axes of the slice: x: 2, y: 2, z: 4, core: 2. Of those that a mesh axis runs over, the one named last changes fastest.
Arguments:
- tokens: bfloat16 [1024, 8192], P('groups', 'tensor'), parts along dimension 0, may hold values from -6 to 6
- gate_weight: bfloat16 [8192, 14336], P(None, 'tensor'), may hold values from -0.0625 to 0.0625
- up_weight: bfloat16 [8192, 14336], P(None, 'tensor'), may hold values from -0.0625 to 0.0625
- down_weight: bfloat16 [14336, 8192], P('tensor'), may hold values from -0.0625 to 0.0625
- gate_shrink: bfloat16 [8, 8192, 64], P(None, 'tensor'), may hold values from -0.0625 to 0.0625
- gate_expand: bfloat16 [8, 64, 14336], P(None, None, 'tensor'), may hold values from -0.75 to 0.75
- up_shrink: bfloat16 [8, 8192, 64], P(None, 'tensor'), may hold values from -0.0625 to 0.0625
- up_expand: bfloat16 [8, 64, 14336], P(None, None, 'tensor'), may hold values from -0.75 to 0.75
- down_first_factor: bfloat16 [8, 14336, 64], P(None, 'tensor'), may hold values from -0.046875 to 0.046875
- down_expand: bfloat16 [8, 64, 8192], P(None, None, 'tensor'), may hold values from -0.75 to 0.75
- block_adapter: int32 [16], P('groups'), parts along dimension 0, may hold values from 0 to 7, as said below
- live_slot_count: int32 [16], P('groups'), parts along dimension 0, may hold values from 1 to 64, as said below
Outputs:
- mixed: bfloat16 [1024, 8192], P('groups', 'tensor'), parts along dimension 0
The draws below stay inside these ranges and needn't reach their ends.
There are 2 independent parts, one for each index of `groups`. The reference program is written for one: setup_inputs(seed, part) draws one part's arguments, and reference() takes and returns one part's arrays. A program takes and returns all parts, laid end to end along the dimension named above; an argument that names none is the same for every part. Nothing has to cross between parts.
Inputs may be any that keep to these rules, and one draw needn't show every extreme that they name: `live_slot_count`: some block is full in every draw. `block_adapter`: every draw names adapter 0 and adapter 8 - 1 in some blocks.
All inputs are finite; a program needn't handle non-finite values.
Results may differ from the reference program's by a relative error of at most 0.0055.
Values may be sent and summed in bfloat16 or wider, within the bound.
A program may use at most 192 MiB of HBM per device.

```python
import jax
import jax.numpy as jnp
from jax import lax

MODEL_WIDTH = 8192
HIDDEN_UNITS = 14336
RANK = 64
ADAPTERS = 8
BLOCK_SLOTS = 64
ROW_BLOCK_TOTAL = 8
TOKENS = 512


def draw_live_slot_count(key, part):
    key = jax.random.fold_in(key, 7)
    draw_key, pick_key = jax.random.split(key)
    slot_counts = jax.random.randint(draw_key, (ROW_BLOCK_TOTAL,), 1, BLOCK_SLOTS + 1)
    complete_block = jax.random.randint(pick_key, (), 0, ROW_BLOCK_TOTAL)
    return jnp.where(jnp.arange(ROW_BLOCK_TOTAL) == complete_block, BLOCK_SLOTS, slot_counts).astype(jnp.int32)


def draw_block_adapter(key, part):
    key = jax.random.fold_in(key, 11)
    draw_key, order_key = jax.random.split(key)
    chosen = jax.random.randint(draw_key, (ROW_BLOCK_TOTAL,), 0, ADAPTERS)
    positions = jnp.arange(ROW_BLOCK_TOTAL)
    chosen = jnp.where(positions == 0, 0, chosen)
    chosen = jnp.where(positions == 1, ADAPTERS - 1, chosen)
    shuffle = jax.random.permutation(order_key, ROW_BLOCK_TOTAL)
    return chosen[shuffle].astype(jnp.int32)


def raised(entries, stream_key, source, target, parts, factor):
    def block_of(position):
        return (jnp.arange(entries.shape[position]) // (entries.shape[position] // parts)).reshape((-1,) + (1,) * (entries.ndim - 1 - position))

    first = jax.random.permutation(stream_key, parts)[block_of(target)]
    second = (block_of(target) + parts // 2) % parts
    return jnp.where((block_of(source) == first) | (block_of(source) == second), factor * entries, entries)


def level_of(rng, extent, pieces, smallest, largest):
    gain, own = 1.0, jax.random.fold_in(rng, 6)
    for axis_at, blocks in pieces:
        draws = jnp.exp(jax.random.uniform(jax.random.fold_in(own, axis_at), (blocks,), jnp.float32, smallest / len(pieces), largest / len(pieces)))
        gain = gain * jnp.repeat(draws, extent[axis_at] // blocks).reshape([-1 if axis == axis_at else 1 for axis in range(len(extent))])
    return gain


def centred(own_key, extent, spread, bound, cuts=(), kind=jnp.bfloat16):
    entries = spread * jax.random.normal(own_key, extent, jnp.float32)
    if cuts:
        entries = entries * level_of(own_key, extent, cuts, -0.22, 0.18)
    return jnp.clip(entries, -bound, bound).astype(kind)


def heavy_noise(stream_key, shape, width, reach, cuts, heavy, dtype=jnp.bfloat16):
    array = width * jax.random.normal(stream_key, shape, jnp.float32)
    if cuts:
        array = array * level_of(stream_key, shape, cuts, -0.22, 0.18)
    return jnp.clip(raised(array, jax.random.fold_in(stream_key, 3), *heavy), -reach, reach).astype(dtype)


def setup_inputs(seed: int = 0, part: int = 0) -> dict:
    key_list = jax.random.split(jax.random.key(seed), 13)
    own_keys = jax.random.split(jax.random.fold_in(key_list[12], part), 13)
    return {
        "tokens": centred(own_keys[0], (TOKENS, MODEL_WIDTH), 1.0, 6.0, ((1, 16),)),
        "gate_weight": centred(key_list[1], (MODEL_WIDTH, HIDDEN_UNITS), MODEL_WIDTH ** -0.5, 0.0625, ((1, 16),)),
        "up_weight": centred(key_list[2], (MODEL_WIDTH, HIDDEN_UNITS), MODEL_WIDTH ** -0.5, 0.0625, ((1, 16),)),
        "down_weight": heavy_noise(key_list[3], (HIDDEN_UNITS, MODEL_WIDTH), HIDDEN_UNITS ** -0.5, 0.0625, ((0, 16),), (0, 1, 16, 2.0)),
        "gate_shrink": centred(key_list[4], (ADAPTERS, MODEL_WIDTH, RANK), MODEL_WIDTH ** -0.5, 0.0625, ((1, 16),)),
        "gate_expand": centred(key_list[5], (ADAPTERS, RANK, HIDDEN_UNITS), RANK ** -0.5, 0.75, ((2, 16),)),
        "up_shrink": centred(key_list[6], (ADAPTERS, MODEL_WIDTH, RANK), MODEL_WIDTH ** -0.5, 0.0625, ((1, 16),)),
        "up_expand": centred(key_list[7], (ADAPTERS, RANK, HIDDEN_UNITS), RANK ** -0.5, 0.75, ((2, 16),)),
        "down_first_factor": centred(key_list[8], (ADAPTERS, HIDDEN_UNITS, RANK), HIDDEN_UNITS ** -0.5, 0.046875, ((1, 16),)),
        "down_expand": centred(key_list[9], (ADAPTERS, RANK, MODEL_WIDTH), RANK ** -0.5, 0.75, ((2, 16),)),
        "block_adapter": draw_block_adapter(jax.random.fold_in(jax.random.fold_in(key_list[12], part), 71), part),
        "live_slot_count": draw_live_slot_count(jax.random.fold_in(jax.random.fold_in(key_list[12], part), 71), part),
    }


SCALE = 0.5


def reference(tokens, gate_weight, up_weight, down_weight, gate_shrink, gate_expand, up_shrink, up_expand, down_first_factor, down_expand, block_adapter, live_slot_count):
    single_block = jnp.float32

    def first_factor_of(left, table):
        raw = jnp.einsum("btk,bkr->btr", left, table[block_adapter].astype(single_block))
        return lax.optimization_barrier(raw.astype(jnp.bfloat16)).astype(single_block)

    def expand_of(lowrank, table):
        return jnp.einsum("btr,brk->btk", lowrank, table[block_adapter].astype(single_block)).reshape(TOKENS, -1)

    token_row_blocks = tokens.reshape(ROW_BLOCK_TOTAL, BLOCK_SLOTS, MODEL_WIDTH).astype(single_block)
    gate_sum = jnp.dot(tokens, gate_weight, preferred_element_type=single_block) + SCALE * expand_of(first_factor_of(token_row_blocks, gate_shrink), gate_expand)
    up_sum = jnp.dot(tokens, up_weight, preferred_element_type=single_block) + SCALE * expand_of(first_factor_of(token_row_blocks, up_shrink), up_expand)
    hidden_units = (jax.nn.silu(gate_sum) * up_sum).astype(jnp.bfloat16)
    adapter_down_term = first_factor_of(hidden_units.reshape(ROW_BLOCK_TOTAL, BLOCK_SLOTS, HIDDEN_UNITS).astype(single_block), down_first_factor)
    full_sum = jnp.dot(hidden_units, down_weight, preferred_element_type=single_block) + SCALE * expand_of(adapter_down_term, down_expand)
    active_rows = lax.broadcasted_iota(jnp.int32, (ROW_BLOCK_TOTAL, BLOCK_SLOTS), 1) < live_slot_count[:, None]
    return jnp.where(active_rows.reshape(TOKENS, 1), full_sum, 0.0).astype(jnp.bfloat16)
```

```python
import functools

import jax
import jax.numpy as jnp
from jax import lax
from jax.experimental import pallas as pl
from jax.experimental.pallas import tpu as pltpu
from jax.sharding import PartitionSpec as P

SCALE = 0.5
LANES = 128
F32 = jnp.float32
BF16 = jnp.bfloat16


class Ring:
    def __init__(self, n):
        self.n, self.chips = n, n // 2
        self.half, self.side = self.chips // 2, self.chips // 2
        self.me = lax.axis_index("tensor")
        self.chip, self.core = lax.div(self.me, 2), lax.rem(self.me, 2)
        far, row = lax.div(self.chip, 2), lax.rem(self.chip, 2)
        self.place = far + row * (2 * self.side - 1 - 2 * far)
        self.sibling = self.chip * 2 + 1 - self.core
        self.next = (self.chip_at(1) * 2 + self.core, self.chip_at(-1) * 2 + self.core)

    def chip_at(self, offset):
        place = lax.rem(self.place + (offset + self.chips), self.chips)
        row = lax.div(place, self.side)
        far = place + row * (2 * self.side - 1 - 2 * place)
        return far * 2 + row

    def peer(self, step):
        return lax.rem(self.me + step, self.n)

    def sends(self, way, k, h):
        return k < self.half or (k == self.half and h == way)


def greet(ring):
    barrier = pltpu.get_barrier_semaphore()

    def tell(step, carry):
        pl.semaphore_signal(barrier, inc=1, device_id={"tensor": ring.peer(step)}, device_id_type=pl.DeviceIdType.MESH)
        return carry

    lax.fori_loop(1, ring.n, tell, 0)
    pl.semaphore_wait(barrier, ring.n - 1)


def remote(src, dst, send, recv, device):
    return pltpu.make_async_remote_copy(
        src_ref=src, dst_ref=dst, send_sem=send, recv_sem=recv,
        device_id={"tensor": device}, device_id_type=pl.DeviceIdType.MESH,
    )


class Totals:
    def __init__(self, ring, part, arrived, low, sems):
        self.ring, self.part, self.arrived, self.low = ring, part, arrived, low
        self.s1, self.r1, self.s2, self.r2 = sems
        self.rows = part.shape[0] // ring.n

    def rows_of(self, device):
        return pl.ds(pl.multiple_of(device * self.rows, self.rows), self.rows)

    def first(self, step):
        peer = self.ring.peer(step)
        return remote(self.part.at[self.rows_of(peer)], self.arrived.at[step], self.s1.at[step], self.r1.at[step], peer)

    def second(self, step):
        rows = self.low.at[self.rows_of(self.ring.me)]
        return remote(rows, rows, self.s2.at[step], self.r2.at[step], self.ring.peer(step))

    def each(self, do):
        def body(step, carry):
            do(step)
            return carry

        lax.fori_loop(1, self.ring.n, body, 0)

    def scatter(self):
        self.each(lambda step: self.first(step).start())

    def gather(self):
        self.each(lambda step: self.first(step).wait_recv())
        total = self.part[self.rows_of(self.ring.me), :]
        for step in range(1, self.ring.n):
            total = total + self.arrived[step]
        self.low[self.rows_of(self.ring.me), :] = total.astype(BF16)
        self.each(lambda step: self.second(step).start())

    def finish(self):
        def wait(step):
            rows = self.low.at[self.rows_of(self.ring.peer(self.ring.n - step))]
            remote(rows, rows, self.s2.at[step], self.r2.at[step], self.ring.peer(step)).wait_recv()

        self.each(wait)

    def drain(self):
        self.each(lambda step: self.first(step).wait_send())
        self.each(lambda step: self.second(step).wait_send())


def gate_up_kernel(
    n, tok, wg, wu, part, eg, eu, hidden,
    gath, wbuf, acc, arrived, low,
    tok_sem, w_sem, ring_send, ring_recv, sib_send, sib_recv, s1, r1, s2, r2,
):
    ring = Ring(n)
    half, chips, core = ring.half, ring.chips, ring.core
    count, width = tok.shape
    units = wg.shape[1]
    hrows = count // 2
    offsets = [0]
    for k in range(1, half):
        offsets += [-k, k]
    offsets.append(half)
    slot_of = {offset: slot for slot, offset in enumerate(offsets)}

    def cut(offset, c, h):
        return gath.at[ring.chip_at(offset), c, pl.ds(h * hrows, hrows)]

    def weight_copies(slot):
        rows = pl.ds(pl.multiple_of(ring.chip_at(offsets[slot]) * (2 * width), 2 * width), 2 * width)
        return (
            pltpu.make_async_copy(wg.at[rows], wbuf.at[slot, :, pl.ds(0, units)], w_sem.at[slot, 0]),
            pltpu.make_async_copy(wu.at[rows], wbuf.at[slot, :, pl.ds(units, units)], w_sem.at[slot, 1]),
        )

    def away(way, k):
        return -k if way == 0 else k

    def pass_on(way, k, h):
        block = cut(away(way, k - 1), core, h)
        return remote(block, block, ring_send.at[way, k - 1, h], ring_recv.at[way, k - 1, h], ring.next[way])

    def coming(way, k, h):
        block = cut(away(way, k), core, h)
        return remote(block, block, ring_send.at[way, k - 1, h], ring_recv.at[way, k - 1, h], ring.next[way])

    def to_sibling(offset, h, c):
        block, slot = cut(offset, c, h), slot_of[offset]
        return remote(block, block, sib_send.at[slot, h], sib_recv.at[slot, h], ring.sibling)

    def relay(k, h):
        for way in (0, 1):
            if ring.sends(way, k, h):
                coming(way, k, h).wait_recv()
                if ring.sends(way, k + 1, h):
                    pass_on(way, k + 1, h).start()
                to_sibling(half if k == half else away(way, k), h, core).start()

    def multiply(offset):
        slot = slot_of[offset]
        for copy in weight_copies(slot):
            copy.wait()
        for h in (0, 1):
            to_sibling(offset, h, 1 - core).wait_recv()
        chip = ring.chip_at(offset)

        def tile(i, carry):
            lanes = pl.ds(pl.multiple_of(i * 256, 256), 256)
            new = jnp.dot(gath[chip, 0], wbuf[slot, pl.ds(0, width), lanes], preferred_element_type=F32)
            new = new + jnp.dot(gath[chip, 1], wbuf[slot, pl.ds(width, width), lanes], preferred_element_type=F32)
            if slot == 0:
                acc[:, lanes] = new
            else:
                acc[:, lanes] = acc[:, lanes] + new
            return carry

        lax.fori_loop(0, 2 * units // 256, tile, 0)

    own = pltpu.make_async_copy(tok, gath.at[ring.chip, core], tok_sem)
    own.start()
    for slot in range(chips):
        for copy in weight_copies(slot):
            copy.start()
    totals = Totals(ring, part, arrived, low, (s1, r1, s2, r2))
    greet(ring)
    own.wait()
    totals.scatter()
    for h in (0, 1):
        for way in (0, 1):
            pass_on(way, 1, h).start()
        to_sibling(0, h, core).start()
    multiply(0)
    relay(1, 0)
    totals.gather()
    relay(1, 1)
    for k in range(2, half + 1):
        if k < half:
            relay(k, 0)
            multiply(1 - k)
            relay(k, 1)
            multiply(k - 1)
        else:
            multiply(1 - k)
            relay(k, 0)
            relay(k, 1)
            multiply(k - 1)
    totals.finish()
    multiply(half)

    brows = count // eg.shape[0]

    def block(b, carry):
        rows = pl.ds(pl.multiple_of(b * brows, brows), brows)
        lowb = low[rows, :]
        gate = acc[rows, pl.ds(0, units)] + SCALE * jnp.dot(lowb, eg[b], preferred_element_type=F32)
        up = acc[rows, pl.ds(units, units)] + SCALE * jnp.dot(lowb, eu[b], preferred_element_type=F32)
        hidden[rows, :] = (gate / (1.0 + jnp.exp(-gate)) * up).astype(BF16)
        return carry

    lax.fori_loop(0, eg.shape[0], block, 0)
    totals.drain()
    for k in range(1, half + 1):
        for way in (0, 1):
            for h in (0, 1):
                if ring.sends(way, k, h):
                    pass_on(way, k, h).wait_send()
    for offset in offsets:
        for h in (0, 1):
            to_sibling(offset, h, core).wait_send()


def down_kernel(
    n, hidden, wd, first, expand, live, out,
    wbuf, own, sib_out, sib_in, chain_out, chain_in, part, arrived, low,
    w_sem, ring_send, ring_recv, sib_send, sib_recv, s1, r1, s2, r2,
):
    ring = Ring(n)
    half, chips, core = ring.half, ring.chips, ring.core
    count, width = out.shape
    hrows = count // 2
    blocks = first.shape[0]
    brows = count // blocks
    offsets = [half]
    for k in range(half - 1, 0, -1):
        offsets += [k, -k]
    offsets.append(0)
    slot_of = {offset: slot for slot, offset in enumerate(offsets)}

    def weight_copy(slot, mine):
        device = ring.chip_at(offsets[slot]) * 2 + (core if mine == 0 else 1 - core)
        lanes = pl.ds(pl.multiple_of(device * width, width), width)
        return pltpu.make_async_copy(wd.at[:, lanes], wbuf.at[slot, mine], w_sem.at[slot, mine])

    def half_rows(h):
        return pl.ds(h * hrows, hrows)

    def to_sibling(slot):
        return remote(sib_out.at[slot], sib_in.at[slot], sib_send.at[slot], sib_recv.at[slot], ring.sibling)

    def chain(way, k, h):
        return remote(
            chain_out.at[way, k - 1, half_rows(h)], chain_in.at[way, k - 1, half_rows(h)],
            ring_send.at[way, k - 1, h], ring_recv.at[way, k - 1, h], ring.next[way],
        )

    def multiply(offset):
        slot = slot_of[offset]
        for mine in (1, 0):
            weight_copy(slot, mine).wait()

            def tile(i, carry):
                lanes = pl.ds(pl.multiple_of(i * LANES * step, LANES * step), LANES * step)
                new = jnp.dot(hidden[...], wbuf[slot, mine, :, lanes], preferred_element_type=F32)
                if mine:
                    sib_out[slot, :, lanes] = new.astype(BF16)
                else:
                    own[slot, :, lanes] = new
                return carry

            step = 2 if width % 256 == 0 else 1
            lax.fori_loop(0, width // (LANES * step), tile, 0)
            if mine:
                to_sibling(slot).start()

    def send(k, h):
        for way in (0, 1):
            if not ring.sends(way, k, h):
                continue
            slot = slot_of[half if k == half else (k if way == 0 else -k)]
            rows = half_rows(h)
            total = own[slot, rows, :] + sib_in[slot, rows, :].astype(F32)
            if ring.sends(way, k + 1, h):
                chain(way, k + 1, h).wait_recv()
                total = total + chain_in[way, k, rows, :].astype(F32)
            chain_out[way, k - 1, rows, :] = total.astype(BF16)
            chain(way, k, h).start()

    def await_sibling(*some):
        for offset in some:
            to_sibling(slot_of[offset]).wait_recv()

    for slot in range(chips):
        for mine in (1, 0):
            weight_copy(slot, mine).start()

    def shrink(b, carry):
        rows = pl.ds(pl.multiple_of(b * brows, brows), brows)
        part[rows, :] = jnp.dot(hidden[rows, :], first[b], preferred_element_type=F32)
        return carry

    lax.fori_loop(0, blocks, shrink, 0)
    totals = Totals(ring, part, arrived, low, (s1, r1, s2, r2))
    greet(ring)
    multiply(half)
    totals.scatter()
    await_sibling(half)
    send(half, 0)
    send(half, 1)
    for k in range(half - 1, 0, -1):
        multiply(k)
        multiply(-k)
        await_sibling(k, -k)
        if k == half - 1:
            totals.gather()
        send(k, 0)
        if k == 1:
            multiply(0)
        send(k, 1)
    totals.finish()
    await_sibling(0)
    last = slot_of[0]

    def join(h):
        for way in (0, 1):
            chain(way, 1, h).wait_recv()

        def block(i, carry):
            b = i + h * (blocks // 2)
            rows = pl.ds(pl.multiple_of(b * brows, brows), brows)
            total = own[last, rows, :] + sib_in[last, rows, :].astype(F32)
            total = total + chain_in[0, 0, rows, :].astype(F32) + chain_in[1, 0, rows, :].astype(F32)
            total = total + SCALE * jnp.dot(low[rows, :], expand[b], preferred_element_type=F32)
            out[rows, :] = (total * live[rows, :]).astype(BF16)
            return carry

        lax.fori_loop(0, blocks // 2, block, 0)

    join(0)
    join(1)
    totals.drain()
    for k in range(1, half + 1):
        for way in (0, 1):
            for h in (0, 1):
                if ring.sends(way, k, h):
                    chain(way, k, h).wait_send()
    for slot in range(chips):
        to_sibling(slot).wait_send()


def fused_gate_up(n, tok, wg, wu, part, eg, eu):
    count, width = tok.shape
    units = wg.shape[1]
    chips, half = n // 2, n // 4
    dma = pltpu.SemaphoreType.DMA
    return pl.pallas_call(
        functools.partial(gate_up_kernel, n),
        out_shape=jax.ShapeDtypeStruct((count, units), BF16),
        in_specs=[pl.BlockSpec(memory_space=pl.ANY)] * 3 + [pl.BlockSpec(memory_space=pltpu.VMEM)] * 3,
        out_specs=pl.BlockSpec(memory_space=pltpu.VMEM),
        scratch_shapes=[
            pltpu.VMEM((chips, 2, count, width), BF16),
            pltpu.VMEM((chips, 2 * width, 2 * units), BF16),
            pltpu.VMEM((count, 2 * units), F32),
            pltpu.VMEM((n, count // n, LANES), F32),
            pltpu.VMEM((count, LANES), BF16),
            dma, dma((chips, 2)), dma((2, half, 2)), dma((2, half, 2)), dma((chips, 2)), dma((chips, 2)),
            dma((n,)), dma((n,)), dma((n,)), dma((n,)),
        ],
        compiler_params=pltpu.CompilerParams(
            collective_id=0, has_side_effects=True, vmem_limit_bytes=56 * 2**20
        ),
        name="gather_gate_up",
    )(tok, wg, wu, part, eg, eu)


def fused_down(n, hidden, wd, first, expand, live):
    count, units = hidden.shape
    width = expand.shape[2]
    chips, half = n // 2, n // 4
    dma = pltpu.SemaphoreType.DMA
    return pl.pallas_call(
        functools.partial(down_kernel, n),
        out_shape=jax.ShapeDtypeStruct((count, width), BF16),
        in_specs=[pl.BlockSpec(memory_space=pltpu.VMEM), pl.BlockSpec(memory_space=pl.ANY)]
        + [pl.BlockSpec(memory_space=pltpu.VMEM)] * 3,
        out_specs=pl.BlockSpec(memory_space=pltpu.VMEM),
        scratch_shapes=[
            pltpu.VMEM((chips, 2, units, width), BF16),
            pltpu.VMEM((chips, count, width), F32),
            pltpu.VMEM((chips, count, width), BF16),
            pltpu.VMEM((chips, count, width), BF16),
            pltpu.VMEM((2, half, count, width), BF16),
            pltpu.VMEM((2, half, count, width), BF16),
            pltpu.VMEM((count, LANES), F32),
            pltpu.VMEM((n, count // n, LANES), F32),
            pltpu.VMEM((count, LANES), BF16),
            dma((chips, 2)), dma((2, half, 2)), dma((2, half, 2)), dma((chips,)), dma((chips,)),
            dma((n,)), dma((n,)), dma((n,)), dma((n,)),
        ],
        compiler_params=pltpu.CompilerParams(
            collective_id=1, has_side_effects=True, vmem_limit_bytes=56 * 2**20
        ),
        name="down_scatter",
    )(hidden, wd, first, expand, live)


def kernel_local(
    n, tokens, gate_weight, up_weight, down_weight, gate_shrink, gate_expand, up_shrink, up_expand,
    down_first_factor, down_expand, block_adapter, live_slot_count,
):
    count, width = tokens.shape
    blocks = block_adapter.shape[0]
    brows = count // blocks
    rank = gate_shrink.shape[2]
    held = LANES - rank
    shrink = jnp.concatenate([gate_shrink[block_adapter], up_shrink[block_adapter]], axis=2)
    part = jnp.einsum(
        "btd,bdr->btr", tokens.reshape(blocks, brows, width), shrink, preferred_element_type=F32
    ).reshape(count, 2 * rank)
    below, above = ((0, 0), (0, held), (0, 0)), ((0, 0), (held, 0), (0, 0))
    eg = jnp.pad(gate_expand[block_adapter], below)
    eu = jnp.pad(up_expand[block_adapter], above)
    first = jnp.pad(down_first_factor[block_adapter], ((0, 0), (0, 0), (0, held)))
    expand = jnp.pad(down_expand[block_adapter], below)
    active = lax.broadcasted_iota(jnp.int32, (blocks, brows), 1) < live_slot_count[:, None]
    live = active.reshape(count, 1).astype(F32)
    hidden = fused_gate_up(n, tokens, gate_weight, up_weight, part, eg, eu)
    return fused_down(n, hidden, down_weight, first, expand, live)


def fits(n, tokens, gate_weight, gate_shrink, block_adapter):
    count, width = tokens.shape
    units = gate_weight.shape[1]
    return (
        n % 4 == 0 and n >= 8 and count % (16 * n) == 0 and width % LANES == 0 and units % LANES == 0
        and 2 * gate_shrink.shape[2] == LANES and block_adapter.shape[0] % 2 == 0
        and (count // block_adapter.shape[0]) % 16 == 0
    )


def per_block(left, table, adapter_ids, form):
    return jnp.einsum(form, left, table[adapter_ids], preferred_element_type=jnp.float32)


def plain_local(
    tokens,
    gate_weight,
    up_weight,
    down_weight,
    gate_shrink,
    gate_expand,
    up_shrink,
    up_expand,
    down_first_factor,
    down_expand,
    block_adapter,
    live_slot_count,
):
    token_count, width_dev = tokens.shape
    num_blocks = block_adapter.shape[0]
    row_length = token_count // num_blocks
    ff_dev = gate_weight.shape[1]
    token_row_blocks = tokens.reshape(num_blocks, row_length, width_dev)
    part_gate = per_block(token_row_blocks, gate_shrink, block_adapter, "btd,bdr->btr")
    part_up = per_block(token_row_blocks, up_shrink, block_adapter, "btd,bdr->btr")
    sum_gate, sum_up = lax.psum((part_gate, part_up), "tensor")
    low_gate = sum_gate.astype(jnp.bfloat16)
    low_up = sum_up.astype(jnp.bfloat16)
    columns = lax.all_gather(tokens, "tensor", axis=1, tiled=True)
    gate_sum = jnp.dot(columns, gate_weight, preferred_element_type=jnp.float32)
    up_sum = jnp.dot(columns, up_weight, preferred_element_type=jnp.float32)
    gate_sum = gate_sum + SCALE * per_block(
        low_gate, gate_expand, block_adapter, "btr,brf->btf"
    ).reshape(token_count, ff_dev)
    up_sum = up_sum + SCALE * per_block(low_up, up_expand, block_adapter, "btr,brf->btf").reshape(
        token_count, ff_dev
    )
    hidden_units = (jax.nn.silu(gate_sum) * up_sum).astype(jnp.bfloat16)
    hidden_blocks = hidden_units.reshape(num_blocks, row_length, ff_dev)
    part_down = per_block(hidden_blocks, down_first_factor, block_adapter, "btf,bfr->btr").reshape(
        token_count, -1
    )
    rank_width = part_down.shape[1]
    sum_down = lax.psum(part_down, "tensor")
    base_part = jnp.dot(hidden_units, down_weight, preferred_element_type=jnp.float32)
    own_cols = lax.psum_scatter(base_part, "tensor", scatter_dimension=1, tiled=True)
    adapter_down_term = sum_down.astype(jnp.bfloat16).reshape(num_blocks, row_length, rank_width)
    adapter_term = per_block(adapter_down_term, down_expand, block_adapter, "btr,brd->btd")
    active_rows = (
        lax.broadcasted_iota(jnp.int32, (num_blocks, row_length), 1) < live_slot_count[:, None]
    )
    result = own_cols.reshape(num_blocks, row_length, -1) + SCALE * adapter_term
    return (
        jnp.where(active_rows[:, :, None], result, 0.0)
        .astype(jnp.bfloat16)
        .reshape(token_count, -1)
    )


def solution(mesh):
    placed = (
        P("groups", "tensor"),
        P(None, "tensor"),
        P(None, "tensor"),
        P("tensor", None),
        P(None, "tensor", None),
        P(None, None, "tensor"),
        P(None, "tensor", None),
        P(None, None, "tensor"),
        P(None, "tensor", None),
        P(None, None, "tensor"),
        P("groups"),
        P("groups"),
    )
    n = mesh.shape["tensor"]

    def local(*args):
        if fits(n, args[0], args[1], args[4], args[10]):
            return kernel_local(n, *args)
        return plain_local(*args)

    return jax.shard_map(
        local, mesh=mesh, in_specs=placed, out_specs=P("groups", "tensor"), check_vma=False
    )
```

```python
import functools

import jax
import jax.numpy as jnp
from jax import lax
from jax.experimental import pallas as pl
from jax.experimental.pallas import tpu as pltpu
from jax.sharding import PartitionSpec as P

SCALE = 0.5
LANES = 128
F32 = jnp.float32
BF16 = jnp.bfloat16


class Ring:
    def __init__(self, n):
        self.n, self.chips = n, n // 2
        self.half, self.side = self.chips // 2, self.chips // 2
        self.me = lax.axis_index("tensor")
        self.chip, self.core = lax.div(self.me, 2), lax.rem(self.me, 2)
        far, row = lax.div(self.chip, 2), lax.rem(self.chip, 2)
        self.place = far + row * (2 * self.side - 1 - 2 * far)
        self.sibling = self.chip * 2 + 1 - self.core
        self.next = (self.chip_at(1) * 2 + self.core, self.chip_at(-1) * 2 + self.core)

    def chip_at(self, offset):
        place = lax.rem(self.place + (offset + self.chips), self.chips)
        row = lax.div(place, self.side)
        far = place + row * (2 * self.side - 1 - 2 * place)
        return far * 2 + row

    def peer(self, step):
        return lax.rem(self.me + step, self.n)

    def sends(self, way, k, h):
        return k < self.half or (k == self.half and h == way)


def greet(ring):
    barrier = pltpu.get_barrier_semaphore()

    def tell(step, carry):
        pl.semaphore_signal(barrier, inc=1, device_id={"tensor": ring.peer(step)}, device_id_type=pl.DeviceIdType.MESH)
        return carry

    lax.fori_loop(1, ring.n, tell, 0)
    pl.semaphore_wait(barrier, ring.n - 1)


def remote(src, dst, send, recv, device):
    return pltpu.make_async_remote_copy(
        src_ref=src, dst_ref=dst, send_sem=send, recv_sem=recv,
        device_id={"tensor": device}, device_id_type=pl.DeviceIdType.MESH,
    )


def across(left, right):
    return lax.dot_general(left, right, (((1,), (1,)), ((), ())), preferred_element_type=F32)


class Totals:
    def __init__(self, ring, part, arrived, low, sems):
        self.ring, self.part, self.arrived, self.low = ring, part, arrived, low
        self.s1, self.r1, self.s2, self.r2 = sems
        self.rows = part.shape[0] // ring.n

    def rows_of(self, device):
        return pl.ds(pl.multiple_of(device * self.rows, self.rows), self.rows)

    def first(self, step):
        peer = self.ring.peer(step)
        return remote(self.part.at[self.rows_of(peer)], self.arrived.at[step], self.s1.at[step], self.r1.at[step], peer)

    def second(self, step):
        rows = self.low.at[self.rows_of(self.ring.me)]
        return remote(rows, rows, self.s2.at[step], self.r2.at[step], self.ring.peer(step))

    def each(self, do):
        def body(step, carry):
            do(step)
            return carry

        lax.fori_loop(1, self.ring.n, body, 0)

    def scatter(self):
        self.each(lambda step: self.first(step).start())

    def gather(self):
        self.each(lambda step: self.first(step).wait_recv())
        total = self.part[self.rows_of(self.ring.me), :]
        for step in range(1, self.ring.n):
            total = total + self.arrived[step]
        self.low[self.rows_of(self.ring.me), :] = total.astype(BF16)
        self.each(lambda step: self.second(step).start())

    def finish(self):
        def wait(step):
            rows = self.low.at[self.rows_of(self.ring.peer(self.ring.n - step))]
            remote(rows, rows, self.s2.at[step], self.r2.at[step], self.ring.peer(step)).wait_recv()

        self.each(wait)

    def drain(self):
        self.each(lambda step: self.first(step).wait_send())
        self.each(lambda step: self.second(step).wait_send())


def gate_up_kernel(
    n, adapters, tok, wg, wu, gs, us, ge, ue, hidden,
    gath, wbuf, acc, shrinks, expands, part, arrived, low,
    tok_sem, table_sem, w_sem, ring_send, ring_recv, sib_send, sib_recv, s1, r1, s2, r2,
):
    ring = Ring(n)
    half, chips, core = ring.half, ring.chips, ring.core
    count, width = tok.shape
    units = wg.shape[1]
    hrows = count // 2
    offsets = [0]
    for k in range(1, half):
        offsets += [-k, k]
    offsets.append(half)
    slot_of = {offset: slot for slot, offset in enumerate(offsets)}

    def cut(offset, c, h):
        return gath.at[ring.chip_at(offset), c, pl.ds(h * hrows, hrows)]

    def weight_copies(slot):
        rows = pl.ds(pl.multiple_of(ring.chip_at(offsets[slot]) * (2 * width), 2 * width), 2 * width)
        return (
            pltpu.make_async_copy(wg.at[rows], wbuf.at[slot, :, pl.ds(0, units)], w_sem.at[slot, 0]),
            pltpu.make_async_copy(wu.at[rows], wbuf.at[slot, :, pl.ds(units, units)], w_sem.at[slot, 1]),
        )

    def away(way, k):
        return -k if way == 0 else k

    def pass_on(way, k, h):
        block = cut(away(way, k - 1), core, h)
        return remote(block, block, ring_send.at[way, k - 1, h], ring_recv.at[way, k - 1, h], ring.next[way])

    def coming(way, k, h):
        block = cut(away(way, k), core, h)
        return remote(block, block, ring_send.at[way, k - 1, h], ring_recv.at[way, k - 1, h], ring.next[way])

    def to_sibling(offset, h, c):
        block, slot = cut(offset, c, h), slot_of[offset]
        return remote(block, block, sib_send.at[slot, h], sib_recv.at[slot, h], ring.sibling)

    def relay(k, h):
        for way in (0, 1):
            if ring.sends(way, k, h):
                coming(way, k, h).wait_recv()
                if ring.sends(way, k + 1, h):
                    pass_on(way, k + 1, h).start()
                to_sibling(half if k == half else away(way, k), h, core).start()

    def multiply(offset):
        slot = slot_of[offset]
        for copy in weight_copies(slot):
            copy.wait()
        for h in (0, 1):
            to_sibling(offset, h, 1 - core).wait_recv()
        chip = ring.chip_at(offset)

        def tile(i, carry):
            lanes = pl.ds(pl.multiple_of(i * 256, 256), 256)
            new = jnp.dot(gath[chip, 0], wbuf[slot, pl.ds(0, width), lanes], preferred_element_type=F32)
            new = new + jnp.dot(gath[chip, 1], wbuf[slot, pl.ds(width, width), lanes], preferred_element_type=F32)
            if slot == 0:
                acc[:, lanes] = new
            else:
                acc[:, lanes] = acc[:, lanes] + new
            return carry

        lax.fori_loop(0, 2 * units // 256, tile, 0)

    blocks = adapters.shape[0]
    brows = count // blocks
    own = pltpu.make_async_copy(tok, gath.at[ring.chip, core], tok_sem)
    own.start()
    tables = [
        pltpu.make_async_copy(table, held.at[i], table_sem.at[j])
        for j, (table, held, i) in enumerate(((gs, shrinks, 0), (us, shrinks, 1), (ge, expands, 0), (ue, expands, 1)))
    ]
    for copy in tables:
        copy.start()
    for slot in range(chips):
        for copy in weight_copies(slot):
            copy.start()
    totals = Totals(ring, part, arrived, low, (s1, r1, s2, r2))
    greet(ring)
    own.wait()
    for h in (0, 1):
        for way in (0, 1):
            pass_on(way, 1, h).start()
        to_sibling(0, h, core).start()
    for copy in tables:
        copy.wait()

    def shrink(b, carry):
        rows = pl.ds(pl.multiple_of(b * brows, brows), brows)
        both = jnp.concatenate([shrinks[0, adapters[b]], shrinks[1, adapters[b]]], axis=0)
        part[rows, :] = across(gath[ring.chip, core, rows, :], both)
        return carry

    lax.fori_loop(0, blocks, shrink, 0)
    totals.scatter()
    multiply(0)
    relay(1, 0)
    totals.gather()
    relay(1, 1)
    for k in range(2, half + 1):
        if k < half:
            relay(k, 0)
            multiply(1 - k)
            relay(k, 1)
            multiply(k - 1)
        else:
            multiply(1 - k)
            relay(k, 0)
            relay(k, 1)
            multiply(k - 1)
    totals.finish()
    multiply(half)

    def block(b, carry):
        rows = pl.ds(pl.multiple_of(b * brows, brows), brows)
        lowb = low[rows, :]
        of_gate, of_up = expands[0, adapters[b]], expands[1, adapters[b]]
        blank = jnp.zeros_like(of_gate)
        of_gate, of_up = jnp.concatenate([of_gate, blank], axis=0), jnp.concatenate([blank, of_up], axis=0)
        gate = acc[rows, pl.ds(0, units)] + SCALE * jnp.dot(lowb, of_gate, preferred_element_type=F32)
        up = acc[rows, pl.ds(units, units)] + SCALE * jnp.dot(lowb, of_up, preferred_element_type=F32)
        hidden[rows, :] = (gate / (1.0 + jnp.exp(-gate)) * up).astype(BF16)
        return carry

    lax.fori_loop(0, blocks, block, 0)
    totals.drain()
    for k in range(1, half + 1):
        for way in (0, 1):
            for h in (0, 1):
                if ring.sends(way, k, h):
                    pass_on(way, k, h).wait_send()
    for offset in offsets:
        for h in (0, 1):
            to_sibling(offset, h, core).wait_send()


def down_kernel(
    n, adapters, live, hidden, wd, first, expand, out,
    wbuf, own, sib_out, sib_in, chain_out, chain_in, part, arrived, low,
    w_sem, ring_send, ring_recv, sib_send, sib_recv, s1, r1, s2, r2,
):
    ring = Ring(n)
    half, chips, core = ring.half, ring.chips, ring.core
    count, width = out.shape
    hrows = count // 2
    blocks = adapters.shape[0]
    brows = count // blocks
    offsets = [half]
    for k in range(half - 1, 0, -1):
        offsets += [k, -k]
    offsets.append(0)
    slot_of = {offset: slot for slot, offset in enumerate(offsets)}

    def weight_copy(slot, mine):
        device = ring.chip_at(offsets[slot]) * 2 + (core if mine == 0 else 1 - core)
        lanes = pl.ds(pl.multiple_of(device * width, width), width)
        return pltpu.make_async_copy(wd.at[:, lanes], wbuf.at[slot, mine], w_sem.at[slot, mine])

    def half_rows(h):
        return pl.ds(h * hrows, hrows)

    def to_sibling(slot):
        return remote(sib_out.at[slot], sib_in.at[slot], sib_send.at[slot], sib_recv.at[slot], ring.sibling)

    def chain(way, k, h):
        return remote(
            chain_out.at[way, k - 1, half_rows(h)], chain_in.at[way, k - 1, half_rows(h)],
            ring_send.at[way, k - 1, h], ring_recv.at[way, k - 1, h], ring.next[way],
        )

    def multiply(offset):
        slot = slot_of[offset]
        for mine in (1, 0):
            weight_copy(slot, mine).wait()

            def tile(i, carry):
                lanes = pl.ds(pl.multiple_of(i * LANES * step, LANES * step), LANES * step)
                new = jnp.dot(hidden[...], wbuf[slot, mine, :, lanes], preferred_element_type=F32)
                if mine:
                    sib_out[slot, :, lanes] = new.astype(BF16)
                else:
                    own[slot, :, lanes] = new
                return carry

            step = 2 if width % 256 == 0 else 1
            lax.fori_loop(0, width // (LANES * step), tile, 0)
            if mine:
                to_sibling(slot).start()

    def send(k, h):
        for way in (0, 1):
            if not ring.sends(way, k, h):
                continue
            slot = slot_of[half if k == half else (k if way == 0 else -k)]
            rows = half_rows(h)
            total = own[slot, rows, :] + sib_in[slot, rows, :].astype(F32)
            if ring.sends(way, k + 1, h):
                chain(way, k + 1, h).wait_recv()
                total = total + chain_in[way, k, rows, :].astype(F32)
            chain_out[way, k - 1, rows, :] = total.astype(BF16)
            chain(way, k, h).start()

    def await_sibling(*some):
        for offset in some:
            to_sibling(slot_of[offset]).wait_recv()

    for slot in range(chips):
        for mine in (1, 0):
            weight_copy(slot, mine).start()

    def shrink(b, carry):
        rows = pl.ds(pl.multiple_of(b * brows, brows), brows)
        factor = first[adapters[b]]
        part[rows, :] = across(hidden[rows, :], jnp.concatenate([factor, jnp.zeros_like(factor)], axis=0))
        return carry

    lax.fori_loop(0, blocks, shrink, 0)
    totals = Totals(ring, part, arrived, low, (s1, r1, s2, r2))
    greet(ring)
    multiply(half)
    totals.scatter()
    await_sibling(half)
    send(half, 0)
    send(half, 1)
    for k in range(half - 1, 0, -1):
        multiply(k)
        multiply(-k)
        await_sibling(k, -k)
        if k == half - 1:
            totals.gather()
        send(k, 0)
        if k == 1:
            multiply(0)
        send(k, 1)
    totals.finish()
    await_sibling(0)
    last = slot_of[0]

    def join(h):
        for way in (0, 1):
            chain(way, 1, h).wait_recv()

        def block(i, carry):
            b = i + h * (blocks // 2)
            rows = pl.ds(pl.multiple_of(b * brows, brows), brows)
            total = own[last, rows, :] + sib_in[last, rows, :].astype(F32)
            total = total + chain_in[0, 0, rows, :].astype(F32) + chain_in[1, 0, rows, :].astype(F32)
            factor = expand[adapters[b]]
            factor = jnp.concatenate([factor, jnp.zeros_like(factor)], axis=0)
            total = total + SCALE * jnp.dot(low[rows, :], factor, preferred_element_type=F32)
            active = lax.broadcasted_iota(jnp.int32, total.shape, 0) < live[b]
            out[rows, :] = jnp.where(active, total, 0.0).astype(BF16)
            return carry

        lax.fori_loop(0, blocks // 2, block, 0)

    join(0)
    join(1)
    totals.drain()
    for k in range(1, half + 1):
        for way in (0, 1):
            for h in (0, 1):
                if ring.sends(way, k, h):
                    chain(way, k, h).wait_send()
    for slot in range(chips):
        to_sibling(slot).wait_send()


def fused_gate_up(n, adapters, tok, wg, wu, gs, us, ge, ue):
    count, width = tok.shape
    units = wg.shape[1]
    chips, half = n // 2, n // 4
    dma = pltpu.SemaphoreType.DMA
    return pl.pallas_call(
        functools.partial(gate_up_kernel, n),
        out_shape=jax.ShapeDtypeStruct((count, units), BF16),
        in_specs=[pl.BlockSpec(memory_space=pltpu.SMEM)] + [pl.BlockSpec(memory_space=pl.ANY)] * 7,
        out_specs=pl.BlockSpec(memory_space=pltpu.VMEM),
        scratch_shapes=[
            pltpu.VMEM((chips, 2, count, width), BF16),
            pltpu.VMEM((chips, 2 * width, 2 * units), BF16),
            pltpu.VMEM((count, 2 * units), F32),
            pltpu.VMEM((2, *gs.shape), BF16),
            pltpu.VMEM((2, *ge.shape), BF16),
            pltpu.VMEM((count, LANES), F32),
            pltpu.VMEM((n, count // n, LANES), F32),
            pltpu.VMEM((count, LANES), BF16),
            dma, dma((4,)), dma((chips, 2)), dma((2, half, 2)), dma((2, half, 2)), dma((chips, 2)), dma((chips, 2)),
            dma((n,)), dma((n,)), dma((n,)), dma((n,)),
        ],
        compiler_params=pltpu.CompilerParams(
            collective_id=0, has_side_effects=True, vmem_limit_bytes=56 * 2**20
        ),
        name="gather_gate_up",
    )(adapters, tok, wg, wu, gs, us, ge, ue)


def fused_down(n, adapters, live, hidden, wd, first, expand):
    count, units = hidden.shape
    width = expand.shape[2]
    chips, half = n // 2, n // 4
    dma = pltpu.SemaphoreType.DMA
    return pl.pallas_call(
        functools.partial(down_kernel, n),
        out_shape=jax.ShapeDtypeStruct((count, width), BF16),
        in_specs=[pl.BlockSpec(memory_space=pltpu.SMEM)] * 2
        + [pl.BlockSpec(memory_space=pltpu.VMEM), pl.BlockSpec(memory_space=pl.ANY)]
        + [pl.BlockSpec(memory_space=pltpu.VMEM)] * 2,
        out_specs=pl.BlockSpec(memory_space=pltpu.VMEM),
        scratch_shapes=[
            pltpu.VMEM((chips, 2, units, width), BF16),
            pltpu.VMEM((chips, count, width), F32),
            pltpu.VMEM((chips, count, width), BF16),
            pltpu.VMEM((chips, count, width), BF16),
            pltpu.VMEM((2, half, count, width), BF16),
            pltpu.VMEM((2, half, count, width), BF16),
            pltpu.VMEM((count, LANES), F32),
            pltpu.VMEM((n, count // n, LANES), F32),
            pltpu.VMEM((count, LANES), BF16),
            dma((chips, 2)), dma((2, half, 2)), dma((2, half, 2)), dma((chips,)), dma((chips,)),
            dma((n,)), dma((n,)), dma((n,)), dma((n,)),
        ],
        compiler_params=pltpu.CompilerParams(
            collective_id=1, has_side_effects=True, vmem_limit_bytes=56 * 2**20
        ),
        name="down_scatter",
    )(adapters, live, hidden, wd, first, expand)


def kernel_local(
    n, tokens, gate_weight, up_weight, down_weight, gate_shrink, gate_expand, up_shrink, up_expand,
    down_first_factor, down_expand, block_adapter, live_slot_count,
):
    def turned(table):
        return jnp.swapaxes(table, 1, 2)

    hidden = fused_gate_up(
        n, block_adapter, tokens, gate_weight, up_weight, turned(gate_shrink), turned(up_shrink), gate_expand, up_expand
    )
    return fused_down(n, block_adapter, live_slot_count, hidden, down_weight, turned(down_first_factor), down_expand)


def fits(n, tokens, gate_weight, gate_shrink, block_adapter):
    count, width = tokens.shape
    units = gate_weight.shape[1]
    return (
        n % 4 == 0 and n >= 8 and count % (16 * n) == 0 and width % LANES == 0 and units % LANES == 0
        and 2 * gate_shrink.shape[2] == LANES and block_adapter.shape[0] % 2 == 0
        and (count // block_adapter.shape[0]) % 16 == 0
    )


def per_block(left, table, adapter_ids, form):
    return jnp.einsum(form, left, table[adapter_ids], preferred_element_type=jnp.float32)


def plain_local(
    tokens,
    gate_weight,
    up_weight,
    down_weight,
    gate_shrink,
    gate_expand,
    up_shrink,
    up_expand,
    down_first_factor,
    down_expand,
    block_adapter,
    live_slot_count,
):
    token_count, width_dev = tokens.shape
    num_blocks = block_adapter.shape[0]
    row_length = token_count // num_blocks
    ff_dev = gate_weight.shape[1]
    token_row_blocks = tokens.reshape(num_blocks, row_length, width_dev)
    part_gate = per_block(token_row_blocks, gate_shrink, block_adapter, "btd,bdr->btr")
    part_up = per_block(token_row_blocks, up_shrink, block_adapter, "btd,bdr->btr")
    sum_gate, sum_up = lax.psum((part_gate, part_up), "tensor")
    low_gate = sum_gate.astype(jnp.bfloat16)
    low_up = sum_up.astype(jnp.bfloat16)
    columns = lax.all_gather(tokens, "tensor", axis=1, tiled=True)
    gate_sum = jnp.dot(columns, gate_weight, preferred_element_type=jnp.float32)
    up_sum = jnp.dot(columns, up_weight, preferred_element_type=jnp.float32)
    gate_sum = gate_sum + SCALE * per_block(
        low_gate, gate_expand, block_adapter, "btr,brf->btf"
    ).reshape(token_count, ff_dev)
    up_sum = up_sum + SCALE * per_block(low_up, up_expand, block_adapter, "btr,brf->btf").reshape(
        token_count, ff_dev
    )
    hidden_units = (jax.nn.silu(gate_sum) * up_sum).astype(jnp.bfloat16)
    hidden_blocks = hidden_units.reshape(num_blocks, row_length, ff_dev)
    part_down = per_block(hidden_blocks, down_first_factor, block_adapter, "btf,bfr->btr").reshape(
        token_count, -1
    )
    rank_width = part_down.shape[1]
    sum_down = lax.psum(part_down, "tensor")
    base_part = jnp.dot(hidden_units, down_weight, preferred_element_type=jnp.float32)
    own_cols = lax.psum_scatter(base_part, "tensor", scatter_dimension=1, tiled=True)
    adapter_down_term = sum_down.astype(jnp.bfloat16).reshape(num_blocks, row_length, rank_width)
    adapter_term = per_block(adapter_down_term, down_expand, block_adapter, "btr,brd->btd")
    active_rows = (
        lax.broadcasted_iota(jnp.int32, (num_blocks, row_length), 1) < live_slot_count[:, None]
    )
    result = own_cols.reshape(num_blocks, row_length, -1) + SCALE * adapter_term
    return (
        jnp.where(active_rows[:, :, None], result, 0.0)
        .astype(jnp.bfloat16)
        .reshape(token_count, -1)
    )


def solution(mesh):
    placed = (
        P("groups", "tensor"),
        P(None, "tensor"),
        P(None, "tensor"),
        P("tensor", None),
        P(None, "tensor", None),
        P(None, None, "tensor"),
        P(None, "tensor", None),
        P(None, None, "tensor"),
        P(None, "tensor", None),
        P(None, None, "tensor"),
        P("groups"),
        P("groups"),
    )
    n = mesh.shape["tensor"]

    def local(*args):
        if fits(n, args[0], args[1], args[4], args[10]):
            return kernel_local(n, *args)
        return plain_local(*args)

    return jax.shard_map(
        local, mesh=mesh, in_specs=placed, out_specs=P("groups", "tensor"), check_vma=False
    )
```

```python
import functools

import jax
import jax.numpy as jnp
from jax import lax
from jax.experimental import pallas as pl
from jax.experimental.pallas import tpu as pltpu
from jax.sharding import PartitionSpec as P

SCALE = 0.5
LANES = 128
F32 = jnp.float32
BF16 = jnp.bfloat16


class Ring:
    def __init__(self, n):
        self.n, self.chips = n, n // 2
        self.half, self.side = self.chips // 2, self.chips // 2
        self.me = lax.axis_index("tensor")
        self.chip, self.core = lax.div(self.me, 2), lax.rem(self.me, 2)
        far, row = lax.div(self.chip, 2), lax.rem(self.chip, 2)
        self.place = far + row * (2 * self.side - 1 - 2 * far)
        self.sibling = self.chip * 2 + 1 - self.core
        self.next = (self.chip_at(1) * 2 + self.core, self.chip_at(-1) * 2 + self.core)

    def chip_at(self, offset):
        place = lax.rem(self.place + (offset + self.chips), self.chips)
        row = lax.div(place, self.side)
        far = place + row * (2 * self.side - 1 - 2 * place)
        return far * 2 + row

    def peer_chip(self, step):
        return lax.rem(self.chip + step, self.chips)

    def sends(self, way, k, h):
        return k < self.half or (k == self.half and h == way)


def greet(ring):
    barrier = pltpu.get_barrier_semaphore()

    def greet_device(device):
        pl.semaphore_signal(barrier, inc=1, device_id={"tensor": device}, device_id_type=pl.DeviceIdType.MESH)

    def tell(step, carry):
        greet_device(ring.peer_chip(step) * 2 + ring.core)
        return carry

    greet_device(ring.sibling)
    lax.fori_loop(1, ring.chips, tell, 0)
    pl.semaphore_wait(barrier, ring.chips)


def remote(src, dst, send, recv, device):
    return pltpu.make_async_remote_copy(
        src_ref=src, dst_ref=dst, send_sem=send, recv_sem=recv,
        device_id={"tensor": device}, device_id_type=pl.DeviceIdType.MESH,
    )


def across(left, right):
    return lax.dot_general(left, right, (((1,), (1,)), ((), ())), preferred_element_type=F32)


class Totals:
    def __init__(self, ring, part, beside, mid, arrived, low, sems):
        self.ring, self.part, self.beside, self.mid, self.arrived, self.low = ring, part, beside, mid, arrived, low
        self.s0, self.r0, self.s1, self.r1, self.s2, self.r2 = sems
        self.held = part.shape[0] // 2
        self.rows = self.held // ring.chips

    def half_of(self, core):
        return pl.ds(pl.multiple_of(core * self.held, self.held), self.held)

    def rows_of(self, chip):
        return pl.ds(pl.multiple_of(chip * self.rows, self.rows), self.rows)

    def low_of(self, chip):
        return self.low.at[pl.ds(pl.multiple_of(self.ring.core * self.held + chip * self.rows, self.rows), self.rows)]

    def peer(self, step):
        chip = self.ring.peer_chip(step)
        return chip, chip * 2 + self.ring.core

    def pairing(self):
        rows = self.part.at[self.half_of(1 - self.ring.core)]
        return remote(rows, self.beside, self.s0.at[0], self.r0.at[0], self.ring.sibling)

    def sharing(self, core):
        rows = self.low.at[self.half_of(core)]
        return remote(rows, rows, self.s0.at[1], self.r0.at[1], self.ring.sibling)

    def first(self, step):
        chip, device = self.peer(step)
        return remote(self.mid.at[self.rows_of(chip)], self.arrived.at[step], self.s1.at[step], self.r1.at[step], device)

    def second(self, step):
        rows = self.low_of(self.ring.chip)
        return remote(rows, rows, self.s2.at[step], self.r2.at[step], self.peer(step)[1])

    def each(self, do):
        def body(step, carry):
            do(step)
            return carry

        lax.fori_loop(1, self.ring.chips, body, 0)

    def pair(self):
        self.pairing().start()

    def scatter(self):
        self.pairing().wait_recv()
        self.beside[...] = self.beside[...] + self.part[self.half_of(self.ring.core), :]
        self.mid[...] = self.beside[...].astype(BF16)
        self.each(lambda step: self.first(step).start())

    def gather(self):
        self.each(lambda step: self.first(step).wait_recv())
        total = self.beside[self.rows_of(self.ring.chip), :]
        for step in range(1, self.ring.chips):
            total = total + self.arrived[step].astype(F32)
        start = pl.multiple_of(self.ring.core * self.held + self.ring.chip * self.rows, self.rows)
        self.low[pl.ds(start, self.rows), :] = total.astype(BF16)
        self.each(lambda step: self.second(step).start())

    def share(self):
        def wait(step):
            rows = self.low_of(self.ring.peer_chip(self.ring.chips - step))
            remote(rows, rows, self.s2.at[step], self.r2.at[step], self.peer(step)[1]).wait_recv()

        self.each(wait)
        self.sharing(self.ring.core).start()

    def finish(self):
        self.sharing(1 - self.ring.core).wait_recv()

    def drain(self):
        self.pairing().wait_send()
        self.each(lambda step: self.first(step).wait_send())
        self.each(lambda step: self.second(step).wait_send())
        self.sharing(self.ring.core).wait_send()

    @staticmethod
    def scratch(rows, chips):
        dma, held = pltpu.SemaphoreType.DMA, rows // 2
        refs = [
            pltpu.VMEM((rows, LANES), F32),
            pltpu.VMEM((held, LANES), F32),
            pltpu.VMEM((held, LANES), BF16),
            pltpu.VMEM((chips, held // chips, LANES), BF16),
            pltpu.VMEM((rows, LANES), BF16),
        ]
        return refs, [dma((2,)), dma((2,))] + [dma((chips,))] * 4


def gate_up_kernel(
    n, adapters, tok, wg, wu, gs, us, ge, ue, hidden,
    gath, wbuf, acc, shrinks, expands, part, beside, mid, arrived, low,
    tok_sem, table_sem, w_sem, ring_send, ring_recv, sib_send, sib_recv, *sems,
):
    ring = Ring(n)
    half, chips, core = ring.half, ring.chips, ring.core
    count, width = tok.shape
    units = wg.shape[1]
    hrows = count // 2
    offsets = [0]
    for k in range(1, half):
        offsets += [-k, k]
    offsets.append(half)
    slot_of = {offset: slot for slot, offset in enumerate(offsets)}

    def cut(offset, c, h):
        return gath.at[ring.chip_at(offset), c, pl.ds(h * hrows, hrows)]

    def weight_copies(slot):
        rows = pl.ds(pl.multiple_of(ring.chip_at(offsets[slot]) * (2 * width), 2 * width), 2 * width)
        return (
            pltpu.make_async_copy(wg.at[rows], wbuf.at[slot, :, pl.ds(0, units)], w_sem.at[slot, 0]),
            pltpu.make_async_copy(wu.at[rows], wbuf.at[slot, :, pl.ds(units, units)], w_sem.at[slot, 1]),
        )

    def away(way, k):
        return -k if way == 0 else k

    def pass_on(way, k, h):
        block = cut(away(way, k - 1), core, h)
        return remote(block, block, ring_send.at[way, k - 1, h], ring_recv.at[way, k - 1, h], ring.next[way])

    def coming(way, k, h):
        block = cut(away(way, k), core, h)
        return remote(block, block, ring_send.at[way, k - 1, h], ring_recv.at[way, k - 1, h], ring.next[way])

    def to_sibling(offset, h, c):
        block, slot = cut(offset, c, h), slot_of[offset]
        return remote(block, block, sib_send.at[slot, h], sib_recv.at[slot, h], ring.sibling)

    def relay(k, h):
        for way in (0, 1):
            if ring.sends(way, k, h):
                coming(way, k, h).wait_recv()
                if ring.sends(way, k + 1, h):
                    pass_on(way, k + 1, h).start()
                to_sibling(half if k == half else away(way, k), h, core).start()

    def multiply(offset):
        slot = slot_of[offset]
        for copy in weight_copies(slot):
            copy.wait()
        for h in (0, 1):
            to_sibling(offset, h, 1 - core).wait_recv()
        chip = ring.chip_at(offset)

        def tile(i, carry):
            lanes = pl.ds(pl.multiple_of(i * 256, 256), 256)
            new = jnp.dot(gath[chip, 0], wbuf[slot, pl.ds(0, width), lanes], preferred_element_type=F32)
            new = new + jnp.dot(gath[chip, 1], wbuf[slot, pl.ds(width, width), lanes], preferred_element_type=F32)
            if slot == 0:
                acc[:, lanes] = new
            else:
                acc[:, lanes] = acc[:, lanes] + new
            return carry

        lax.fori_loop(0, 2 * units // 256, tile, 0)

    blocks = adapters.shape[0]
    brows = count // blocks
    own = pltpu.make_async_copy(tok, gath.at[ring.chip, core], tok_sem)
    own.start()
    tables = [
        pltpu.make_async_copy(table, held.at[i], table_sem.at[j])
        for j, (table, held, i) in enumerate(((gs, shrinks, 0), (us, shrinks, 1), (ge, expands, 0), (ue, expands, 1)))
    ]
    for copy in tables:
        copy.start()
    for slot in range(chips):
        for copy in weight_copies(slot):
            copy.start()
    totals = Totals(ring, part, beside, mid, arrived, low, sems)
    greet(ring)
    own.wait()
    for h in (0, 1):
        for way in (0, 1):
            pass_on(way, 1, h).start()
        to_sibling(0, h, core).start()
    for copy in tables:
        copy.wait()

    def shrink(b, carry):
        rows = pl.ds(pl.multiple_of(b * brows, brows), brows)
        both = jnp.concatenate([shrinks[0, adapters[b]], shrinks[1, adapters[b]]], axis=0)
        part[rows, :] = across(gath[ring.chip, core, rows, :], both)
        return carry

    lax.fori_loop(0, blocks, shrink, 0)
    totals.pair()
    totals.scatter()
    multiply(0)
    relay(1, 0)
    relay(1, 1)
    totals.gather()
    for k in range(2, half + 1):
        if k < half:
            relay(k, 0)
            multiply(1 - k)
            relay(k, 1)
            multiply(k - 1)
        else:
            totals.share()
            multiply(1 - k)
            relay(k, 0)
            relay(k, 1)
            multiply(k - 1)
    totals.finish()
    multiply(half)

    def block(b, carry):
        rows = pl.ds(pl.multiple_of(b * brows, brows), brows)
        lowb = low[rows, :]
        of_gate, of_up = expands[0, adapters[b]], expands[1, adapters[b]]
        blank = jnp.zeros_like(of_gate)
        of_gate, of_up = jnp.concatenate([of_gate, blank], axis=0), jnp.concatenate([blank, of_up], axis=0)
        gate = acc[rows, pl.ds(0, units)] + SCALE * jnp.dot(lowb, of_gate, preferred_element_type=F32)
        up = acc[rows, pl.ds(units, units)] + SCALE * jnp.dot(lowb, of_up, preferred_element_type=F32)
        hidden[rows, :] = (gate / (1.0 + jnp.exp(-gate)) * up).astype(BF16)
        return carry

    lax.fori_loop(0, blocks, block, 0)
    totals.drain()
    for k in range(1, half + 1):
        for way in (0, 1):
            for h in (0, 1):
                if ring.sends(way, k, h):
                    pass_on(way, k, h).wait_send()
    for offset in offsets:
        for h in (0, 1):
            to_sibling(offset, h, core).wait_send()


def down_kernel(
    n, adapters, live, hidden, wd, first, expand, out,
    wbuf, own, sib_out, sib_in, chain_out, chain_in, part, beside, mid, arrived, low,
    w_sem, ring_send, ring_recv, sib_send, sib_recv, *sems,
):
    ring = Ring(n)
    half, chips, core = ring.half, ring.chips, ring.core
    count, width = out.shape
    hrows = count // 2
    blocks = adapters.shape[0]
    brows = count // blocks
    offsets = [half]
    for k in range(half - 1, 0, -1):
        offsets += [k, -k]
    offsets.append(0)
    slot_of = {offset: slot for slot, offset in enumerate(offsets)}

    def weight_copy(slot, mine):
        device = ring.chip_at(offsets[slot]) * 2 + (core if mine == 0 else 1 - core)
        lanes = pl.ds(pl.multiple_of(device * width, width), width)
        return pltpu.make_async_copy(wd.at[:, lanes], wbuf.at[slot, mine], w_sem.at[slot, mine])

    def half_rows(h):
        return pl.ds(h * hrows, hrows)

    def to_sibling(slot):
        return remote(sib_out.at[slot], sib_in.at[slot], sib_send.at[slot], sib_recv.at[slot], ring.sibling)

    def chain(way, k, h):
        return remote(
            chain_out.at[way, k - 1, half_rows(h)], chain_in.at[way, k - 1, half_rows(h)],
            ring_send.at[way, k - 1, h], ring_recv.at[way, k - 1, h], ring.next[way],
        )

    def multiply(offset):
        slot = slot_of[offset]
        for mine in (1, 0):
            weight_copy(slot, mine).wait()

            def tile(i, carry):
                lanes = pl.ds(pl.multiple_of(i * LANES * step, LANES * step), LANES * step)
                new = jnp.dot(hidden[...], wbuf[slot, mine, :, lanes], preferred_element_type=F32)
                if mine:
                    sib_out[slot, :, lanes] = new.astype(BF16)
                else:
                    own[slot, :, lanes] = new
                return carry

            step = 2 if width % 256 == 0 else 1
            lax.fori_loop(0, width // (LANES * step), tile, 0)
            if mine:
                to_sibling(slot).start()

    def send(k, h):
        for way in (0, 1):
            if not ring.sends(way, k, h):
                continue
            slot = slot_of[half if k == half else (k if way == 0 else -k)]
            rows = half_rows(h)
            total = own[slot, rows, :] + sib_in[slot, rows, :].astype(F32)
            if ring.sends(way, k + 1, h):
                chain(way, k + 1, h).wait_recv()
                total = total + chain_in[way, k, rows, :].astype(F32)
            chain_out[way, k - 1, rows, :] = total.astype(BF16)
            chain(way, k, h).start()

    def await_sibling(*some):
        for offset in some:
            to_sibling(slot_of[offset]).wait_recv()

    for slot in range(chips):
        for mine in (1, 0):
            weight_copy(slot, mine).start()

    def shrink(b, carry):
        rows = pl.ds(pl.multiple_of(b * brows, brows), brows)
        lower = pl.ds(pl.multiple_of(hrows + b * brows, brows), brows)
        factor, other = first[adapters[b]], first[adapters[b + blocks // 2]]
        blank = jnp.zeros_like(factor)
        left = across(hidden[rows, :], jnp.concatenate([factor, blank], axis=0))
        part[rows, :] = left + across(hidden[lower, :], jnp.concatenate([blank, other], axis=0))
        return carry

    lax.fori_loop(0, blocks // 2, shrink, 0)
    totals = Totals(ring, part, beside, mid, arrived, low, sems)
    greet(ring)
    totals.pair()
    multiply(half)
    totals.scatter()
    await_sibling(half)
    send(half, 0)
    send(half, 1)
    for k in range(half - 1, 0, -1):
        multiply(k)
        multiply(-k)
        await_sibling(k, -k)
        if k == half - 1:
            totals.gather()
        send(k, 0)
        if k == 1:
            multiply(0)
        send(k, 1)
    totals.share()
    totals.finish()
    await_sibling(0)
    last = slot_of[0]

    def join(h):
        for way in (0, 1):
            chain(way, 1, h).wait_recv()

        def block(i, carry):
            b = i + h * (blocks // 2)
            rows = pl.ds(pl.multiple_of(b * brows, brows), brows)
            total = own[last, rows, :] + sib_in[last, rows, :].astype(F32)
            total = total + chain_in[0, 0, rows, :].astype(F32) + chain_in[1, 0, rows, :].astype(F32)
            factor = expand[adapters[b]]
            pieces = [factor, jnp.zeros_like(factor)]
            factor = jnp.concatenate(pieces if h == 0 else pieces[::-1], axis=0)
            packed = pl.ds(pl.multiple_of(i * brows, brows), brows)
            total = total + SCALE * jnp.dot(low[packed, :], factor, preferred_element_type=F32)
            active = lax.broadcasted_iota(jnp.int32, total.shape, 0) < live[b]
            out[rows, :] = jnp.where(active, total, 0.0).astype(BF16)
            return carry

        lax.fori_loop(0, blocks // 2, block, 0)

    join(0)
    join(1)
    totals.drain()
    for k in range(1, half + 1):
        for way in (0, 1):
            for h in (0, 1):
                if ring.sends(way, k, h):
                    chain(way, k, h).wait_send()
    for slot in range(chips):
        to_sibling(slot).wait_send()


def fused_gate_up(n, adapters, tok, wg, wu, gs, us, ge, ue):
    count, width = tok.shape
    units = wg.shape[1]
    chips, half = n // 2, n // 4
    dma = pltpu.SemaphoreType.DMA
    refs, sems = Totals.scratch(count, chips)
    return pl.pallas_call(
        functools.partial(gate_up_kernel, n),
        out_shape=jax.ShapeDtypeStruct((count, units), BF16),
        in_specs=[pl.BlockSpec(memory_space=pltpu.SMEM)] + [pl.BlockSpec(memory_space=pl.ANY)] * 7,
        out_specs=pl.BlockSpec(memory_space=pltpu.VMEM),
        scratch_shapes=[
            pltpu.VMEM((chips, 2, count, width), BF16),
            pltpu.VMEM((chips, 2 * width, 2 * units), BF16),
            pltpu.VMEM((count, 2 * units), F32),
            pltpu.VMEM((2, *gs.shape), BF16),
            pltpu.VMEM((2, *ge.shape), BF16),
            *refs,
            dma, dma((4,)), dma((chips, 2)), dma((2, half, 2)), dma((2, half, 2)), dma((chips, 2)), dma((chips, 2)),
            *sems,
        ],
        compiler_params=pltpu.CompilerParams(
            collective_id=0, has_side_effects=True, vmem_limit_bytes=56 * 2**20
        ),
        name="gather_gate_up",
    )(adapters, tok, wg, wu, gs, us, ge, ue)


def fused_down(n, adapters, live, hidden, wd, first, expand):
    count, units = hidden.shape
    width = expand.shape[2]
    chips, half = n // 2, n // 4
    dma = pltpu.SemaphoreType.DMA
    refs, sems = Totals.scratch(count // 2, chips)
    return pl.pallas_call(
        functools.partial(down_kernel, n),
        out_shape=jax.ShapeDtypeStruct((count, width), BF16),
        in_specs=[pl.BlockSpec(memory_space=pltpu.SMEM)] * 2
        + [pl.BlockSpec(memory_space=pltpu.VMEM), pl.BlockSpec(memory_space=pl.ANY)]
        + [pl.BlockSpec(memory_space=pltpu.VMEM)] * 2,
        out_specs=pl.BlockSpec(memory_space=pltpu.VMEM),
        scratch_shapes=[
            pltpu.VMEM((chips, 2, units, width), BF16),
            pltpu.VMEM((chips, count, width), F32),
            pltpu.VMEM((chips, count, width), BF16),
            pltpu.VMEM((chips, count, width), BF16),
            pltpu.VMEM((2, half, count, width), BF16),
            pltpu.VMEM((2, half, count, width), BF16),
            *refs,
            dma((chips, 2)), dma((2, half, 2)), dma((2, half, 2)), dma((chips,)), dma((chips,)),
            *sems,
        ],
        compiler_params=pltpu.CompilerParams(
            collective_id=1, has_side_effects=True, vmem_limit_bytes=56 * 2**20
        ),
        name="down_scatter",
    )(adapters, live, hidden, wd, first, expand)


def kernel_local(
    n, tokens, gate_weight, up_weight, down_weight, gate_shrink, gate_expand, up_shrink, up_expand,
    down_first_factor, down_expand, block_adapter, live_slot_count,
):
    def turned(table):
        return jnp.swapaxes(table, 1, 2)

    hidden = fused_gate_up(
        n, block_adapter, tokens, gate_weight, up_weight, turned(gate_shrink), turned(up_shrink), gate_expand, up_expand
    )
    return fused_down(n, block_adapter, live_slot_count, hidden, down_weight, turned(down_first_factor), down_expand)


def fits(n, tokens, gate_weight, gate_shrink, block_adapter):
    count, width = tokens.shape
    units = gate_weight.shape[1]
    return (
        n % 4 == 0 and n >= 8 and count % (32 * n) == 0 and width % LANES == 0 and units % LANES == 0
        and 2 * gate_shrink.shape[2] == LANES and block_adapter.shape[0] % 2 == 0
        and (count // block_adapter.shape[0]) % 16 == 0
    )


def per_block(left, table, adapter_ids, form):
    return jnp.einsum(form, left, table[adapter_ids], preferred_element_type=jnp.float32)


def plain_local(
    tokens,
    gate_weight,
    up_weight,
    down_weight,
    gate_shrink,
    gate_expand,
    up_shrink,
    up_expand,
    down_first_factor,
    down_expand,
    block_adapter,
    live_slot_count,
):
    token_count, width_dev = tokens.shape
    num_blocks = block_adapter.shape[0]
    row_length = token_count // num_blocks
    ff_dev = gate_weight.shape[1]
    token_row_blocks = tokens.reshape(num_blocks, row_length, width_dev)
    part_gate = per_block(token_row_blocks, gate_shrink, block_adapter, "btd,bdr->btr")
    part_up = per_block(token_row_blocks, up_shrink, block_adapter, "btd,bdr->btr")
    sum_gate, sum_up = lax.psum((part_gate, part_up), "tensor")
    low_gate = sum_gate.astype(jnp.bfloat16)
    low_up = sum_up.astype(jnp.bfloat16)
    columns = lax.all_gather(tokens, "tensor", axis=1, tiled=True)
    gate_sum = jnp.dot(columns, gate_weight, preferred_element_type=jnp.float32)
    up_sum = jnp.dot(columns, up_weight, preferred_element_type=jnp.float32)
    gate_sum = gate_sum + SCALE * per_block(
        low_gate, gate_expand, block_adapter, "btr,brf->btf"
    ).reshape(token_count, ff_dev)
    up_sum = up_sum + SCALE * per_block(low_up, up_expand, block_adapter, "btr,brf->btf").reshape(
        token_count, ff_dev
    )
    hidden_units = (jax.nn.silu(gate_sum) * up_sum).astype(jnp.bfloat16)
    hidden_blocks = hidden_units.reshape(num_blocks, row_length, ff_dev)
    part_down = per_block(hidden_blocks, down_first_factor, block_adapter, "btf,bfr->btr").reshape(
        token_count, -1
    )
    rank_width = part_down.shape[1]
    sum_down = lax.psum(part_down, "tensor")
    base_part = jnp.dot(hidden_units, down_weight, preferred_element_type=jnp.float32)
    own_cols = lax.psum_scatter(base_part, "tensor", scatter_dimension=1, tiled=True)
    adapter_down_term = sum_down.astype(jnp.bfloat16).reshape(num_blocks, row_length, rank_width)
    adapter_term = per_block(adapter_down_term, down_expand, block_adapter, "btr,brd->btd")
    active_rows = (
        lax.broadcasted_iota(jnp.int32, (num_blocks, row_length), 1) < live_slot_count[:, None]
    )
    result = own_cols.reshape(num_blocks, row_length, -1) + SCALE * adapter_term
    return (
        jnp.where(active_rows[:, :, None], result, 0.0)
        .astype(jnp.bfloat16)
        .reshape(token_count, -1)
    )


def solution(mesh):
    placed = (
        P("groups", "tensor"),
        P(None, "tensor"),
        P(None, "tensor"),
        P("tensor", None),
        P(None, "tensor", None),
        P(None, None, "tensor"),
        P(None, "tensor", None),
        P(None, None, "tensor"),
        P(None, "tensor", None),
        P(None, None, "tensor"),
        P("groups"),
        P("groups"),
    )
    n = mesh.shape["tensor"]

    def local(*args):
        if fits(n, args[0], args[1], args[4], args[10]):
            return kernel_local(n, *args)
        return plain_local(*args)

    return jax.shard_map(
        local, mesh=mesh, in_specs=placed, out_specs=P("groups", "tensor"), check_vma=False
    )
```
